32 devices in a mesh: parts: 2 (over x), owner: 4 (over y, core), helper: 4 (over z).
Axes of the slice: x: 2, y: 2, z: 4, core: 2. Of those that a mesh axis runs over, the one named last changes fastest.
Arguments:
- embeddings: bfloat16 [32768, 768], P(('parts', 'owner', 'helper')), parts along dimension 0
- cluster_sizes: int32 [64], P('parts'), parts along dimension 0, may hold values from 1 to 4096, 16384 in all
Outputs:
- nearest: float32 [32768], P(('parts', 'owner', 'helper')), parts along dimension 0
The draws below stay inside these ranges and needn't reach their ends.
There are 2 independent parts, one for each index of `parts`. The reference program is written for one: setup_inputs(seed, part) draws one part's arguments, and reference() takes and returns one part's arrays. A program takes and returns all parts, laid end to end along the dimension named above; each array names one. Nothing has to cross between parts.
Inputs may be any that keep to these rules, and one draw needn't show every extreme that they name: `cluster_sizes`: the sizes add up to 16384; the largest is exactly 4096.
All inputs are finite; a program needn't handle non-finite values.
Results may differ from the reference program's by a relative error of at most 0.00053.
Values may be sent and summed in bfloat16 or wider, within the bound.
A program may use at most 64 MiB of HBM per device.

```python
import math
import jax
import jax.numpy as jnp
import numpy as np
from jax import lax

D = 768
ROWS_DEV = 1024
REACH = 4
ROWS = 16384
MOST = 4096
CLUSTERS = 32


def draw_embeddings(key, part):
    key = jax.random.fold_in(key, 7)
    streams = jax.random.split(key, 4)
    centers = jax.random.normal(streams[0], (ROWS // 64, D), jnp.float32)
    members = jax.random.randint(streams[1], (ROWS,), 0, ROWS // 64)
    strength = jax.random.uniform(streams[2], (ROWS, 1), jnp.float32, 0.5, 2.0)
    shared = strength * centers[members]
    noise_part = jax.random.normal(streams[3], (ROWS, D), jnp.float32)
    return (noise_part + shared).astype(jnp.bfloat16)


def split_up(count, total, bound, slope):
    weights = [(1 << 20) // math.isqrt(standing ** slope) + 1 for standing in range(2, count + 1)]
    surplus, given = total - bound - (count - 1), [1] * (count - 1)
    while surplus > 0:
        free = [i for i in range(count - 1) if given[i] < bound]
        whole, left = sum([weights[i] for i in free]), surplus
        for i in free:
            addition = min(bound - given[i], max(1, left * weights[i] // whole), surplus)
            given[i] = given[i] + addition
            surplus = surplus - addition
    return np.array([bound] + given)


def ragged_sizes(rng, count, total, reach, lean):
    if count == 2:
        one = jax.random.randint(rng, (), max(1, total - reach), min(reach, total - 1) + 1)
        return jnp.stack([one, total - one])
    tallies = jnp.asarray(split_up(count, total, reach, lean), jnp.int32)
    couples = (count - 1) // 2
    source_of, receiver = tallies[1:1 + 2 * couples:2], tallies[2:2 + 2 * couples:2]
    slack = jnp.minimum(source_of - 1, reach - receiver)
    moved = jax.random.randint(jax.random.fold_in(rng, 1), (couples,), 0, 1 << 20) % (slack + 1)
    tallies = tallies.at[1:1 + 2 * couples:2].set(source_of - moved).at[2:2 + 2 * couples:2].set(receiver + moved)
    return tallies[jax.random.permutation(jax.random.fold_in(rng, 2), count)]


def setup_inputs(seed: int = 0, part: int = 0) -> dict:
    seeds = jax.random.split(jax.random.key(seed), 3)
    part_keys = jax.random.split(jax.random.fold_in(seeds[2], part), 3)
    return {
        "embeddings": draw_embeddings(jax.random.fold_in(jax.random.fold_in(seeds[2], part), 71), part),
        "cluster_sizes": ragged_sizes(part_keys[1], CLUSTERS, ROWS, MOST, 2).astype(jnp.int32),
    }


FLOOR = -2.0

def normalize(embeddings):
    values = embeddings.astype(jnp.float32)
    factor = lax.rsqrt(lax.optimization_barrier(jnp.mean(values * values, axis=1, keepdims=True)) + 1e-06) * (1.0 / math.sqrt(values.shape[1]))
    return (values * factor).astype(jnp.bfloat16)

def cluster_of(first_row, row_total, cluster_ends):
    positions = first_row + jnp.arange(row_total, dtype=jnp.int32)
    located = lax.optimization_barrier(jnp.sum((positions[:, None] >= cluster_ends[None, :]).astype(jnp.int32), axis=1)).astype(jnp.int32)
    return jnp.where(positions < 0, -1, located).astype(jnp.int32)

def tile_best(row_unit, row_cluster, column_unit, column_cluster, skip_self):
    scores = lax.dot_general(row_unit, column_unit, (((1,), (1,)), ((), ())), preferred_element_type=jnp.float32)
    same_cluster = row_cluster[:, None] == column_cluster[None, :]
    if skip_self:
        row_total = row_unit.shape[0]
        same_cluster = same_cluster & (lax.broadcasted_iota(jnp.int32, (row_total, row_total), 0) != lax.broadcasted_iota(jnp.int32, (row_total, row_total), 1))
    masked = jnp.where(same_cluster, scores, FLOOR)
    return (lax.optimization_barrier(jnp.max(masked, axis=1)), lax.optimization_barrier(jnp.max(masked, axis=0)))

def intersections(row_cluster, column_cluster):
    return (row_cluster[0] <= column_cluster[-1]) & (column_cluster[0] <= row_cluster[-1])

def reference(embeddings, cluster_sizes):
    total_rows = embeddings.shape[0]
    unit_rows = normalize(embeddings)
    cluster_ends = jnp.cumsum(cluster_sizes).astype(jnp.int32)
    margin = REACH * ROWS_DEV
    padded = jnp.pad(unit_rows, ((margin, margin), (0, 0)))

    def block_best(block_index):
        first_row = (block_index * ROWS_DEV).astype(jnp.int32)
        own_rows = lax.dynamic_slice_in_dim(padded, (first_row + margin).astype(jnp.int32), ROWS_DEV, 0)
        own_cluster = cluster_of(first_row, ROWS_DEV, cluster_ends)
        best_score = tile_best(own_rows, own_cluster, own_rows, own_cluster, True)[0]
        blank = jnp.full((ROWS_DEV,), FLOOR, jnp.float32)
        for offset in range(-REACH, REACH + 1):
            if offset == 0:
                continue
            other_first = (first_row + offset * ROWS_DEV).astype(jnp.int32)
            other_rows = lax.dynamic_slice_in_dim(padded, (other_first + margin).astype(jnp.int32), ROWS_DEV, 0)
            other_cluster = cluster_of(other_first, ROWS_DEV, cluster_ends)
            part_best = lax.cond(intersections(own_cluster, other_cluster), lambda: tile_best(own_rows, own_cluster, other_rows, other_cluster, False)[0], lambda: blank)
            best_score = jnp.maximum(best_score, part_best)
        return jnp.maximum(best_score, -1.0)
    return lax.map(block_best, jnp.arange(total_rows // ROWS_DEV, dtype=jnp.int32)).reshape(total_rows)
```

```python
import functools
import math

import jax
import jax.numpy as jnp
from jax import lax
from jax.experimental import pallas as pl
from jax.experimental.pallas import tpu as pltpu
from jax.sharding import PartitionSpec as P

REACH = 4


FLOOR = -2.0


def from_behind(value, axis, steps):
    count = lax.axis_size(axis)
    initial, last = (max(0, -steps), min(count, count - steps))
    return lax.ppermute(value, axis, [(source, source + steps) for source in range(initial, last)])


def normalize(embeddings):
    values = embeddings.astype(jnp.float32)
    factor = lax.rsqrt(jnp.mean(values * values, axis=1, keepdims=True) + 1e-06) * (
        1.0 / math.sqrt(values.shape[1])
    )
    return (values * factor).astype(jnp.bfloat16)


def cluster_of(first_row, row_total, cluster_ends):
    positions = first_row + jnp.arange(row_total, dtype=jnp.int32)
    located = jnp.sum((positions[:, None] >= cluster_ends[None, :]).astype(jnp.int32), axis=1)
    return jnp.where(positions < 0, -1, located)


def tile_best(row_unit, row_cluster, column_unit, column_cluster, skip_self):
    scores = lax.dot_general(
        row_unit, column_unit, (((1,), (1,)), ((), ())), preferred_element_type=jnp.float32
    )
    same_cluster = row_cluster[:, None] == column_cluster[None, :]
    if skip_self:
        row_total = row_unit.shape[0]
        same_cluster = same_cluster & (
            lax.broadcasted_iota(jnp.int32, (row_total, row_total), 0)
            != lax.broadcasted_iota(jnp.int32, (row_total, row_total), 1)
        )
    masked = jnp.where(same_cluster, scores, FLOOR)
    return (jnp.max(masked, axis=1), jnp.max(masked, axis=0))


def intersections(row_cluster, column_cluster):
    return (row_cluster[0] <= column_cluster[-1]) & (column_cluster[0] <= row_cluster[-1])


def body(embeddings, cluster_sizes):
    unit_rows = normalize(embeddings)
    row_total = unit_rows.shape[0]
    cluster_ends = jnp.cumsum(cluster_sizes)
    device_index = lax.axis_index(("owner", "helper"))
    first_row = device_index * row_total
    own_cluster = cluster_of(first_row, row_total, cluster_ends)
    best_score, unused = tile_best(unit_rows, own_cluster, unit_rows, own_cluster, True)
    blank = jnp.full((row_total,), FLOOR, jnp.float32)
    for offset in range(1, REACH + 1):
        lower_rows = from_behind(unit_rows, ("owner", "helper"), offset)
        lower_cluster = cluster_of(first_row - offset * row_total, row_total, cluster_ends)
        lower_best = lax.cond(
            intersections(own_cluster, lower_cluster),
            lambda: tile_best(unit_rows, own_cluster, lower_rows, lower_cluster, False)[0],
            lambda: blank,
        )
        best_score = jnp.maximum(best_score, lower_best)
        upper_rows = from_behind(unit_rows, ("owner", "helper"), -offset)
        upper_cluster = cluster_of(first_row + offset * row_total, row_total, cluster_ends)
        upper_best = lax.cond(
            intersections(own_cluster, upper_cluster),
            lambda: tile_best(unit_rows, own_cluster, upper_rows, upper_cluster, False)[0],
            lambda: blank,
        )
        best_score = jnp.maximum(best_score, upper_best)
    return jnp.maximum(best_score, -1.0)


CHUNK = 256
MESH = pl.DeviceIdType.MESH


def kernel(line, u_ref, slot_ids, own_ids, res_ids, part_ids, out_ref,
           stream, part, row_best, res_best, part_best, own_best, message, returned, part_back,
           own_send, own_recv, part_send, part_recv, flow_send, ret_send, ret_recv, pb_send, pb_recv):
    rows = u_ref.shape[0]
    chunks = rows // CHUNK
    o, z = lax.axis_index("owner"), lax.axis_index("helper")
    middle = ((o + 1) // 2) % 2
    held = o + middle * (3 - 2 * o)
    sibling = o + 1 - 2 * (o % 2)
    ahead = 2 * (o % 2) - 1
    is_middle = middle == 1

    barrier = pltpu.get_barrier_semaphore()

    def greet(owner, helper):
        pl.semaphore_signal(barrier, inc=1, device_id={"owner": owner, "helper": helper}, device_id_type=MESH)

    for step in range(1, line):
        greet(o, lax.rem(z + step, line))
    greet(sibling, z)

    @pl.when(is_middle)
    def _():
        for helper in range(line):
            greet(3 - o, jnp.int32(helper))
        pl.semaphore_wait(barrier, 2 * line)

    @pl.when(jnp.logical_not(is_middle))
    def _():
        pl.semaphore_wait(barrier, line)

    def piece(c):
        return pl.ds(pl.multiple_of(c * CHUNK, CHUNK), CHUNK)

    def swap(c):
        return pltpu.make_async_remote_copy(
            src_ref=u_ref.at[piece(c)], dst_ref=stream.at[z, piece(c)],
            send_sem=own_send.at[c], recv_sem=own_recv.at[z, c],
            device_id={"owner": 3 - o, "helper": z}, device_id_type=MESH)

    def keep(c):
        return pltpu.make_async_copy(u_ref.at[piece(c)], stream.at[z, piece(c)], own_recv.at[z, c])

    def flow(slot, c):
        return pltpu.make_async_remote_copy(
            src_ref=stream.at[slot, piece(c)], dst_ref=stream.at[slot, piece(c)],
            send_sem=flow_send.at[slot, c], recv_sem=own_recv.at[slot, c],
            device_id={"owner": o, "helper": z + ahead}, device_id_type=MESH)

    partner = pltpu.make_async_remote_copy(
        src_ref=u_ref, dst_ref=part, send_sem=part_send, recv_sem=part_recv,
        device_id={"owner": sibling, "helper": z}, device_id_type=MESH)
    partner_here = pltpu.make_async_copy(u_ref, part, part_recv)
    has_next = (z + ahead >= 0) & (z + ahead < line)

    @pl.when(is_middle)
    def _():
        for c in range(chunks):
            swap(c).start()
        partner.start()

    @pl.when(jnp.logical_not(is_middle))
    def _():
        for c in range(chunks):
            keep(c).start()

    @pl.when(o == 2)
    def _():
        partner_here.start()

    row_best[...] = jnp.full_like(row_best, FLOOR)
    for ref in (res_best, part_best, own_best):
        ref[...] = jnp.full_like(ref, FLOOR)

    def columns_loop(block, ids, columns_ref, column_ids, best, row_total, diagonal):
        def step(k, row_total):
            at = pl.ds(pl.multiple_of(k * CHUNK, CHUNK), CHUNK)
            scores = lax.dot_general(
                block, columns_ref[at, :], (((1,), (1,)), ((), ())), preferred_element_type=jnp.float32)
            same = ids == column_ids[:, at]
            if diagonal is not None:
                first = lax.broadcasted_iota(jnp.int32, scores.shape, 0) + diagonal * CHUNK
                second = lax.broadcasted_iota(jnp.int32, scores.shape, 1) + k * CHUNK
                same = same & (first != second)
            scores = jnp.where(same, scores, FLOOR)
            best[:, at] = jnp.maximum(best[:, at], jnp.max(scores.reshape(CHUNK // 8, 8, CHUNK), axis=0))
            if row_total is None:
                return None
            return jnp.maximum(row_total, jnp.maximum(scores[:, :128], scores[:, 128:]))

        return lax.fori_loop(0, rows // CHUNK, step, row_total)

    def own_step(c, carry):
        @pl.when(is_middle)
        def _():
            swap(c).wait_recv()

        @pl.when(jnp.logical_not(is_middle))
        def _():
            keep(c).wait()

        @pl.when(has_next)
        def _():
            flow(z, c).start()

        return carry

    def self_step(c, carry):
        columns_loop(u_ref[piece(c), :], own_row(c), u_ref, own_ids, own_best, None, c)
        return carry

    def own_row(c):
        return slot_ids[pl.ds(pl.multiple_of(line * rows + c * CHUNK, CHUNK), CHUNK), :]

    def slot_row(slot, c):
        return slot_ids[pl.ds(pl.multiple_of(slot * rows + c * CHUNK, CHUNK), CHUNK), :]

    @pl.when(is_middle)
    def _():
        lax.fori_loop(0, chunks, self_step, 0)

    lax.fori_loop(0, chunks, own_step, 0)

    @pl.when(jnp.logical_not(is_middle))
    def _():
        lax.fori_loop(0, chunks, self_step, 0)
        partner.wait_recv()

    @pl.when(o == 2)
    def _():
        partner_here.wait()

    def with_part(slot, c):
        best = row_best.at[slot, piece(c)]
        best[...] = columns_loop(stream[slot, piece(c), :], slot_row(slot, c), part, part_ids, part_best, best[...], None)

    def part_step(c, carry):
        with_part(z, c)
        return carry

    @pl.when(o != 1)
    def _():
        lax.fori_loop(0, chunks, part_step, 0)

    def to_home(slot):
        return pltpu.make_async_remote_copy(
            src_ref=message.at[slot], dst_ref=returned.at[z],
            send_sem=ret_send.at[slot], recv_sem=ret_recv.at[z],
            device_id={"owner": held, "helper": slot}, device_id_type=MESH)

    def from_holder(helper):
        return pltpu.make_async_remote_copy(
            src_ref=message.at[z], dst_ref=returned.at[helper],
            send_sem=ret_send.at[z], recv_sem=ret_recv.at[helper],
            device_id={"owner": held, "helper": helper}, device_id_type=MESH)

    def folded(slot):
        return jnp.max(row_best[slot].T.reshape(16, 8, rows), axis=0)

    def flow_step(h, carry):
        slot = z - h * ahead

        @pl.when((slot >= 0) & (slot < line))
        def _():
            def chunk_step(c, carry):
                flow(slot, c).wait_recv()

                @pl.when(has_next)
                def _():
                    flow(slot, c).start()

                best = row_best.at[slot, piece(c)]
                best[...] = columns_loop(
                    stream[slot, piece(c), :], slot_row(slot, c), stream.at[z], res_ids, res_best, best[...], None)

                @pl.when(o != 1)
                def _():
                    with_part(slot, c)

                return carry

            lax.fori_loop(0, chunks, chunk_step, 0)
            message[slot] = folded(slot)
            to_home(slot).start()

        return carry

    lax.fori_loop(1, line, flow_step, 0)

    message[z] = jnp.maximum(folded(z), res_best[...])
    part_home = pltpu.make_async_remote_copy(
        src_ref=part_best, dst_ref=part_back, send_sem=pb_send, recv_sem=pb_recv,
        device_id={"owner": sibling, "helper": z}, device_id_type=MESH)

    @pl.when(is_middle)
    def _():
        to_home(z).start()

    @pl.when(jnp.logical_not(is_middle))
    def _():
        part_home.start()
        own_best[...] = jnp.maximum(own_best[...], message[z])

    @pl.when(o == 2)
    def _():
        own_best[...] = jnp.maximum(own_best[...], part_best[...])

    @pl.when(is_middle)
    def _():
        from_holder(z).wait_recv()
        own_best[...] = jnp.maximum(own_best[...], returned[z])
        part_home.wait_recv()
        own_best[...] = jnp.maximum(own_best[...], part_back[...])

    back = 2 * (held % 2) - 1

    def collect(h, carry):
        helper = z + h * back

        @pl.when((helper >= 0) & (helper < line))
        def _():
            from_holder(helper).wait_recv()
            own_best[...] = jnp.maximum(own_best[...], returned[helper])

        slot = z - h * ahead

        @pl.when((slot >= 0) & (slot < line))
        def _():
            to_home(slot).wait_send()

        return carry

    lax.fori_loop(1, line, collect, 0)
    out_ref[...] = jnp.maximum(jnp.max(own_best[...], axis=0, keepdims=True), -1.0)

    @pl.when(is_middle)
    def _():
        to_home(z).wait_send()
        for c in range(chunks):
            swap(c).wait_send()
        partner.wait_send()

    @pl.when(jnp.logical_not(is_middle))
    def _():
        part_home.wait_send()

    @pl.when(has_next)
    def _():
        def drain(h, carry):
            slot = z - h * ahead

            @pl.when((slot >= 0) & (slot < line))
            def _():
                for c in range(chunks):
                    flow(slot, c).wait_send()

            return carry

        lax.fori_loop(0, line, drain, 0)


def chain_body(line, embeddings, cluster_sizes):
    unit_rows = normalize(embeddings)
    rows, width = unit_rows.shape
    ends = jnp.cumsum(cluster_sizes)
    o, z = lax.axis_index("owner"), lax.axis_index("helper")
    held = jnp.where((o == 1) | (o == 2), 3 - o, o)
    ids = lambda block, total: cluster_of(block * rows, total, ends)
    own_ids = ids(o * line + z, rows)
    slot_ids = jnp.concatenate([ids(held * line, rows * line), own_ids])[:, None]
    res_ids = ids(held * line + z, rows)[None]
    part_ids = ids(jnp.where(o == 0, 1, 2) * line + z, rows)[None]
    chunks = rows // CHUNK
    best = pl.pallas_call(
        functools.partial(kernel, line),
        out_shape=jax.ShapeDtypeStruct((1, rows), jnp.float32),
        in_specs=[pl.BlockSpec(memory_space=pltpu.VMEM)] * 5,
        out_specs=pl.BlockSpec(memory_space=pltpu.VMEM),
        scratch_shapes=[
            pltpu.VMEM((line, rows, width), jnp.bfloat16),
            pltpu.VMEM((rows, width), jnp.bfloat16),
            pltpu.VMEM((line, rows, 128), jnp.float32),
            pltpu.VMEM((8, rows), jnp.float32),
            pltpu.VMEM((8, rows), jnp.float32),
            pltpu.VMEM((8, rows), jnp.float32),
            pltpu.VMEM((line, 8, rows), jnp.float32),
            pltpu.VMEM((line, 8, rows), jnp.float32),
            pltpu.VMEM((8, rows), jnp.float32),
            pltpu.SemaphoreType.DMA((chunks,)),
            pltpu.SemaphoreType.DMA((line, chunks)),
            pltpu.SemaphoreType.DMA,
            pltpu.SemaphoreType.DMA,
            pltpu.SemaphoreType.DMA((line, chunks)),
            pltpu.SemaphoreType.DMA((line,)),
            pltpu.SemaphoreType.DMA((line,)),
            pltpu.SemaphoreType.DMA,
            pltpu.SemaphoreType.DMA,
        ],
        compiler_params=pltpu.CompilerParams(
            collective_id=0, has_side_effects=True, vmem_limit_bytes=48 * 2**20
        ),
    )(unit_rows, slot_ids, own_ids[None], res_ids, part_ids)
    return best.reshape(rows)


def solution(mesh):
    placed = (P(("parts", "owner", "helper"), None), P("parts"))
    line = mesh.shape["helper"]
    chained = mesh.shape["owner"] == 4 and line == REACH
    return jax.shard_map(
        functools.partial(chain_body, line) if chained else body,
        mesh=mesh, in_specs=placed, out_specs=P(("parts", "owner", "helper")), check_vma=False
    )
```

```python
import functools
import math

import jax
import jax.numpy as jnp
from jax import lax
from jax.experimental import pallas as pl
from jax.experimental.pallas import tpu as pltpu
from jax.sharding import PartitionSpec as P

REACH = 4


FLOOR = -2.0


def from_behind(value, axis, steps):
    count = lax.axis_size(axis)
    initial, last = (max(0, -steps), min(count, count - steps))
    return lax.ppermute(value, axis, [(source, source + steps) for source in range(initial, last)])


def normalize(embeddings):
    values = embeddings.astype(jnp.float32)
    factor = lax.rsqrt(jnp.mean(values * values, axis=1, keepdims=True) + 1e-06) * (
        1.0 / math.sqrt(values.shape[1])
    )
    return (values * factor).astype(jnp.bfloat16)


def cluster_of(first_row, row_total, cluster_ends):
    positions = first_row + jnp.arange(row_total, dtype=jnp.int32)
    located = jnp.sum((positions[:, None] >= cluster_ends[None, :]).astype(jnp.int32), axis=1)
    return jnp.where(positions < 0, -1, located)


def tile_best(row_unit, row_cluster, column_unit, column_cluster, skip_self):
    scores = lax.dot_general(
        row_unit, column_unit, (((1,), (1,)), ((), ())), preferred_element_type=jnp.float32
    )
    same_cluster = row_cluster[:, None] == column_cluster[None, :]
    if skip_self:
        row_total = row_unit.shape[0]
        same_cluster = same_cluster & (
            lax.broadcasted_iota(jnp.int32, (row_total, row_total), 0)
            != lax.broadcasted_iota(jnp.int32, (row_total, row_total), 1)
        )
    masked = jnp.where(same_cluster, scores, FLOOR)
    return (jnp.max(masked, axis=1), jnp.max(masked, axis=0))


def intersections(row_cluster, column_cluster):
    return (row_cluster[0] <= column_cluster[-1]) & (column_cluster[0] <= row_cluster[-1])


def body(embeddings, cluster_sizes):
    unit_rows = normalize(embeddings)
    row_total = unit_rows.shape[0]
    cluster_ends = jnp.cumsum(cluster_sizes)
    device_index = lax.axis_index(("owner", "helper"))
    first_row = device_index * row_total
    own_cluster = cluster_of(first_row, row_total, cluster_ends)
    best_score, unused = tile_best(unit_rows, own_cluster, unit_rows, own_cluster, True)
    blank = jnp.full((row_total,), FLOOR, jnp.float32)
    for offset in range(1, REACH + 1):
        lower_rows = from_behind(unit_rows, ("owner", "helper"), offset)
        lower_cluster = cluster_of(first_row - offset * row_total, row_total, cluster_ends)
        lower_best = lax.cond(
            intersections(own_cluster, lower_cluster),
            lambda: tile_best(unit_rows, own_cluster, lower_rows, lower_cluster, False)[0],
            lambda: blank,
        )
        best_score = jnp.maximum(best_score, lower_best)
        upper_rows = from_behind(unit_rows, ("owner", "helper"), -offset)
        upper_cluster = cluster_of(first_row + offset * row_total, row_total, cluster_ends)
        upper_best = lax.cond(
            intersections(own_cluster, upper_cluster),
            lambda: tile_best(unit_rows, own_cluster, upper_rows, upper_cluster, False)[0],
            lambda: blank,
        )
        best_score = jnp.maximum(best_score, upper_best)
    return jnp.maximum(best_score, -1.0)


CHUNK = 256
MESH = pl.DeviceIdType.MESH


def kernel(line, u_ref, slot_ids, own_ids, res_ids, part_ids, out_ref,
           stream, part, row_best, res_best, part_best, own_best, message, returned, part_back, pair_back,
           out_send, swap_send, own_recv, part_send, part_recv, flow_send, ret_send, ret_recv,
           pb_send, pb_recv, pair_send, pair_recv):
    rows = u_ref.shape[0]
    chunks = rows // CHUNK
    o, z = lax.axis_index("owner"), lax.axis_index("helper")
    middle = ((o + 1) // 2) % 2
    held = o + middle * (3 - 2 * o)
    sibling = o + 1 - 2 * (o % 2)
    near, outer = 1 + z // 2, 3 * (z // 2)
    is_middle, is_end = middle == 1, middle == 0
    is_inner, is_outer = z == near, z == outer
    takes = near == 1 + o % 2
    gives = near != 1 + o % 2

    barrier = pltpu.get_barrier_semaphore()

    def greet(owner, helper):
        pl.semaphore_signal(barrier, inc=1, device_id={"owner": owner, "helper": helper}, device_id_type=MESH)

    for step in range(1, line):
        greet(o, lax.rem(z + step, line))
    for helper in range(line):
        greet(sibling, jnp.int32(helper))

    @pl.when(is_middle)
    def _():
        for helper in range(line):
            greet(3 - o, jnp.int32(helper))
        pl.semaphore_wait(barrier, 3 * line - 1)

    @pl.when(is_end)
    def _():
        pl.semaphore_wait(barrier, 2 * line - 1)

    def piece(c):
        return pl.ds(pl.multiple_of(c * CHUNK, CHUNK), CHUNK)

    def remote(src, dst, send, recv, owner, helper):
        return pltpu.make_async_remote_copy(
            src_ref=src, dst_ref=dst, send_sem=send, recv_sem=recv,
            device_id={"owner": owner, "helper": helper}, device_id_type=MESH)

    def inward_end(c):
        return remote(u_ref.at[piece(c)], stream.at[outer, piece(c)], out_send.at[c], own_recv.at[outer, c], o, near)

    def inward_middle(c):
        return remote(u_ref.at[piece(c)], part.at[1, piece(c)], out_send.at[c], part_recv.at[1, c], o, near)

    def swap_near(c):
        return remote(u_ref.at[piece(c)], stream.at[near, piece(c)], swap_send.at[0, c], own_recv.at[near, c], 3 - o, near)

    def swap_outer(c):
        return remote(part.at[1, piece(c)], stream.at[outer, piece(c)], swap_send.at[1, c], own_recv.at[outer, c], 3 - o, near)

    def share_near(c):
        return remote(u_ref.at[piece(c)], part.at[0, piece(c)], part_send.at[0, c], part_recv.at[0, c], sibling, near)

    def share_outer(c):
        return remote(part.at[1, piece(c)], part.at[1, piece(c)], part_send.at[1, c], part_recv.at[1, c], sibling, near)

    def keep(c):
        return pltpu.make_async_copy(u_ref.at[piece(c)], stream.at[near, piece(c)], own_recv.at[near, c])

    def keep_part(c):
        return pltpu.make_async_copy(u_ref.at[piece(c)], part.at[0, piece(c)], part_recv.at[0, c])

    def flow(slot, c):
        return remote(stream.at[slot, piece(c)], stream.at[slot, piece(c)], flow_send.at[slot, c], own_recv.at[slot, c], o, 3 - near)

    def each_chunk(action):
        def step(c, carry):
            action(c)
            return carry

        lax.fori_loop(0, chunks, step, 0)

    def columns_loop(block, ids, columns_ref, column_ids, best, row_total, diagonal):
        def step(k, row_total):
            at = pl.ds(pl.multiple_of(k * CHUNK, CHUNK), CHUNK)
            scores = lax.dot_general(
                block, columns_ref[at, :], (((1,), (1,)), ((), ())), preferred_element_type=jnp.float32)
            same = ids == column_ids[:, at]
            if diagonal is not None:
                first = lax.broadcasted_iota(jnp.int32, scores.shape, 0) + diagonal * CHUNK
                second = lax.broadcasted_iota(jnp.int32, scores.shape, 1) + k * CHUNK
                same = same & (first != second)
            scores = jnp.where(same, scores, FLOOR)
            best[:, at] = jnp.maximum(best[:, at], jnp.max(scores.reshape(CHUNK // 8, 8, CHUNK), axis=0))
            if row_total is None:
                return None
            return jnp.maximum(row_total, jnp.maximum(scores[:, :128], scores[:, 128:]))

        return lax.fori_loop(0, rows // CHUNK, step, row_total)

    def slot_row(slot, c):
        return slot_ids[pl.ds(pl.multiple_of(slot * rows + c * CHUNK, CHUNK), CHUNK), :]

    def self_chunk(c):
        columns_loop(u_ref[piece(c), :], slot_row(line, c), u_ref, own_ids, own_best, None, c)

    def with_res(slot, c, which):
        best = row_best.at[slot, piece(c)]
        best[...] = columns_loop(
            stream[slot, piece(c), :], slot_row(slot, c), stream.at[near if which == 0 else outer],
            res_ids.at[which:which + 1], res_best.at[which], best[...], None)

    def with_part(slot, c, which):
        best = row_best.at[slot, piece(c)]
        best[...] = columns_loop(
            stream[slot, piece(c), :], slot_row(slot, c), part.at[which],
            part_ids.at[which:which + 1], part_best.at[which], best[...], None)

    def folded(slot):
        return jnp.max(row_best[slot].T.reshape(16, 8, rows), axis=0)

    def to_home(slot):
        return remote(message.at[slot], returned.at[near - 1], ret_send.at[slot], ret_recv.at[near - 1], held, slot)

    def from_holder(which):
        return remote(message.at[z], returned.at[which], ret_send.at[z], ret_recv.at[which], held, near)

    def part_home(which):
        return remote(part_best.at[which], part_back, pb_send.at[which], pb_recv, sibling, near if which == 0 else outer)

    pair_home = remote(part_best.at[1], pair_back, pair_send, pair_recv, o, outer)
    there, there_outer = 3 - near, 3 - outer

    own_best[...] = jnp.full_like(own_best, FLOOR)

    @pl.when(is_outer)
    def _():
        @pl.when(is_end)
        def _():
            each_chunk(lambda c: inward_end(c).start())

        @pl.when(is_middle)
        def _():
            each_chunk(lambda c: inward_middle(c).start())

        each_chunk(self_chunk)

    @pl.when(is_inner)
    def _():
        @pl.when(is_middle)
        def _():
            each_chunk(lambda c: swap_near(c).start())
            each_chunk(lambda c: share_near(c).start())

        @pl.when(is_end)
        def _():
            each_chunk(lambda c: keep(c).start())

        @pl.when(o == 2)
        def _():
            each_chunk(lambda c: keep_part(c).start())

        row_best[...] = jnp.full_like(row_best, FLOOR)
        res_best[...] = jnp.full_like(res_best, FLOOR)
        part_best[...] = jnp.full_like(part_best, FLOOR)

        def first(c):
            @pl.when(is_middle)
            def _():
                swap_near(c).wait_recv()

            @pl.when(is_end)
            def _():
                keep(c).wait()

            @pl.when(gives)
            def _():
                flow(near, c).start()

            @pl.when(is_middle)
            def _():
                inward_middle(c).wait_recv()
                swap_outer(c).start()
                share_outer(c).start()

            @pl.when(is_end)
            def _():
                inward_end(c).wait_recv()

                @pl.when(gives)
                def _():
                    flow(outer, c).start()

            self_chunk(c)

        each_chunk(first)

        def second(c):
            @pl.when(is_middle)
            def _():
                swap_outer(c).wait_recv()

                @pl.when(gives)
                def _():
                    flow(outer, c).start()

            with_res(outer, c, 0)

            @pl.when(takes)
            def _():
                flow(there, c).wait_recv()
                with_res(there, c, 0)

        each_chunk(second)

        @pl.when(is_end)
        def _():
            each_chunk(lambda c: share_near(c).wait_recv())
            each_chunk(lambda c: share_outer(c).wait_recv())

        @pl.when(o == 2)
        def _():
            each_chunk(lambda c: keep_part(c).wait())

        def third(c):
            @pl.when(o != 1)
            def _():
                for which in range(2):
                    with_part(near, c, which)
                    with_part(outer, c, which)

            @pl.when(takes)
            def _():
                with_res(there, c, 1)

                @pl.when(o != 1)
                def _():
                    for which in range(2):
                        with_part(there, c, which)

        each_chunk(third)

        @pl.when(takes)
        def _():
            message[there] = folded(there)
            to_home(there).start()

            def fourth(c):
                flow(there_outer, c).wait_recv()
                for which in range(2):
                    with_res(there_outer, c, which)

                @pl.when(o != 1)
                def _():
                    for which in range(2):
                        with_part(there_outer, c, which)

            each_chunk(fourth)
            message[there_outer] = folded(there_outer)
            to_home(there_outer).start()

        message[outer] = jnp.maximum(folded(outer), res_best[1])
        to_home(outer).start()
        message[near] = jnp.maximum(folded(near), res_best[0])

        @pl.when(is_middle)
        def _():
            to_home(near).start()

        @pl.when(is_end)
        def _():
            part_home(0).start()
            part_home(1).start()
            own_best[...] = jnp.maximum(own_best[...], message[near])

        @pl.when(o == 2)
        def _():
            pair_home.start()
            own_best[...] = jnp.maximum(own_best[...], part_best[0])

    @pl.when(is_outer | is_middle)
    def _():
        from_holder(near - 1).wait_recv()
        own_best[...] = jnp.maximum(own_best[...], returned[near - 1])

    @pl.when(near != 1 + held % 2)
    def _():
        from_holder(2 - near).wait_recv()
        own_best[...] = jnp.maximum(own_best[...], returned[2 - near])

    @pl.when(is_middle)
    def _():
        part_home(0).wait_recv()
        own_best[...] = jnp.maximum(own_best[...], part_back[...])

    @pl.when((o == 2) & is_outer)
    def _():
        pair_home.wait_recv()
        own_best[...] = jnp.maximum(own_best[...], pair_back[...])

    out_ref[...] = jnp.maximum(jnp.max(own_best[...], axis=0, keepdims=True), -1.0)

    @pl.when(is_outer)
    def _():
        each_chunk(lambda c: inward_end(c).wait_send())

    @pl.when(is_inner)
    def _():
        to_home(outer).wait_send()

        @pl.when(takes)
        def _():
            to_home(there).wait_send()
            to_home(there_outer).wait_send()

        @pl.when(gives)
        def _():
            each_chunk(lambda c: flow(near, c).wait_send())
            each_chunk(lambda c: flow(outer, c).wait_send())

        @pl.when(is_middle)
        def _():
            to_home(near).wait_send()
            for copy in (swap_near, swap_outer, share_near, share_outer):
                each_chunk(lambda c, copy=copy: copy(c).wait_send())

        @pl.when(is_end)
        def _():
            part_home(0).wait_send()
            part_home(1).wait_send()

        @pl.when(o == 2)
        def _():
            pair_home.wait_send()


def chain_body(line, embeddings, cluster_sizes):
    unit_rows = normalize(embeddings)
    rows, width = unit_rows.shape
    ends = jnp.cumsum(cluster_sizes)
    o, z = lax.axis_index("owner"), lax.axis_index("helper")
    held = jnp.where((o == 1) | (o == 2), 3 - o, o)
    ids = lambda block, total: cluster_of(block * rows, total, ends)
    own_ids = ids(o * line + z, rows)
    slot_ids = jnp.concatenate([ids(held * line, rows * line), own_ids])[:, None]
    near, outer = 1 + z // 2, 3 * (z // 2)
    shared = jnp.where(o == 0, 1, 2) * line
    res_ids = jnp.stack([ids(held * line + near, rows), ids(held * line + outer, rows)])
    part_ids = jnp.stack([ids(shared + near, rows), ids(shared + outer, rows)])
    chunks = rows // CHUNK
    best = pl.pallas_call(
        functools.partial(kernel, line),
        out_shape=jax.ShapeDtypeStruct((1, rows), jnp.float32),
        in_specs=[pl.BlockSpec(memory_space=pltpu.VMEM)] * 5,
        out_specs=pl.BlockSpec(memory_space=pltpu.VMEM),
        scratch_shapes=[
            pltpu.VMEM((line, rows, width), jnp.bfloat16),
            pltpu.VMEM((2, rows, width), jnp.bfloat16),
            pltpu.VMEM((line, rows, 128), jnp.float32),
            pltpu.VMEM((2, 8, rows), jnp.float32),
            pltpu.VMEM((2, 8, rows), jnp.float32),
            pltpu.VMEM((8, rows), jnp.float32),
            pltpu.VMEM((line, 8, rows), jnp.float32),
            pltpu.VMEM((2, 8, rows), jnp.float32),
            pltpu.VMEM((8, rows), jnp.float32),
            pltpu.VMEM((8, rows), jnp.float32),
            pltpu.SemaphoreType.DMA((chunks,)),
            pltpu.SemaphoreType.DMA((2, chunks)),
            pltpu.SemaphoreType.DMA((line, chunks)),
            pltpu.SemaphoreType.DMA((2, chunks)),
            pltpu.SemaphoreType.DMA((2, chunks)),
            pltpu.SemaphoreType.DMA((line, chunks)),
            pltpu.SemaphoreType.DMA((line,)),
            pltpu.SemaphoreType.DMA((2,)),
            pltpu.SemaphoreType.DMA((2,)),
            pltpu.SemaphoreType.DMA,
            pltpu.SemaphoreType.DMA,
            pltpu.SemaphoreType.DMA,
        ],
        compiler_params=pltpu.CompilerParams(
            collective_id=0, has_side_effects=True, vmem_limit_bytes=48 * 2**20
        ),
    )(unit_rows, slot_ids, own_ids[None], res_ids, part_ids)
    return best.reshape(rows)


def solution(mesh):
    placed = (P(("parts", "owner", "helper"), None), P("parts"))
    line = mesh.shape["helper"]
    chained = mesh.shape["owner"] == 4 and line == REACH
    return jax.shard_map(
        functools.partial(chain_body, line) if chained else body,
        mesh=mesh, in_specs=placed, out_specs=P(("parts", "owner", "helper")), check_vma=False
    )
```

```python
import functools
import math

import jax
import jax.numpy as jnp
from jax import lax
from jax.experimental import pallas as pl
from jax.experimental.pallas import tpu as pltpu
from jax.sharding import PartitionSpec as P

REACH = 4


FLOOR = -2.0


def from_behind(value, axis, steps):
    count = lax.axis_size(axis)
    initial, last = (max(0, -steps), min(count, count - steps))
    return lax.ppermute(value, axis, [(source, source + steps) for source in range(initial, last)])


def normalize(embeddings):
    values = embeddings.astype(jnp.float32)
    factor = lax.rsqrt(jnp.mean(values * values, axis=1, keepdims=True) + 1e-06) * (
        1.0 / math.sqrt(values.shape[1])
    )
    return (values * factor).astype(jnp.bfloat16)


def cluster_of(first_row, row_total, cluster_ends):
    positions = first_row + jnp.arange(row_total, dtype=jnp.int32)
    located = jnp.sum((positions[:, None] >= cluster_ends[None, :]).astype(jnp.int32), axis=1)
    return jnp.where(positions < 0, -1, located)


def tile_best(row_unit, row_cluster, column_unit, column_cluster, skip_self):
    scores = lax.dot_general(
        row_unit, column_unit, (((1,), (1,)), ((), ())), preferred_element_type=jnp.float32
    )
    same_cluster = row_cluster[:, None] == column_cluster[None, :]
    if skip_self:
        row_total = row_unit.shape[0]
        same_cluster = same_cluster & (
            lax.broadcasted_iota(jnp.int32, (row_total, row_total), 0)
            != lax.broadcasted_iota(jnp.int32, (row_total, row_total), 1)
        )
    masked = jnp.where(same_cluster, scores, FLOOR)
    return (jnp.max(masked, axis=1), jnp.max(masked, axis=0))


def intersections(row_cluster, column_cluster):
    return (row_cluster[0] <= column_cluster[-1]) & (column_cluster[0] <= row_cluster[-1])


def body(embeddings, cluster_sizes):
    unit_rows = normalize(embeddings)
    row_total = unit_rows.shape[0]
    cluster_ends = jnp.cumsum(cluster_sizes)
    device_index = lax.axis_index(("owner", "helper"))
    first_row = device_index * row_total
    own_cluster = cluster_of(first_row, row_total, cluster_ends)
    best_score, unused = tile_best(unit_rows, own_cluster, unit_rows, own_cluster, True)
    blank = jnp.full((row_total,), FLOOR, jnp.float32)
    for offset in range(1, REACH + 1):
        lower_rows = from_behind(unit_rows, ("owner", "helper"), offset)
        lower_cluster = cluster_of(first_row - offset * row_total, row_total, cluster_ends)
        lower_best = lax.cond(
            intersections(own_cluster, lower_cluster),
            lambda: tile_best(unit_rows, own_cluster, lower_rows, lower_cluster, False)[0],
            lambda: blank,
        )
        best_score = jnp.maximum(best_score, lower_best)
        upper_rows = from_behind(unit_rows, ("owner", "helper"), -offset)
        upper_cluster = cluster_of(first_row + offset * row_total, row_total, cluster_ends)
        upper_best = lax.cond(
            intersections(own_cluster, upper_cluster),
            lambda: tile_best(unit_rows, own_cluster, upper_rows, upper_cluster, False)[0],
            lambda: blank,
        )
        best_score = jnp.maximum(best_score, upper_best)
    return jnp.maximum(best_score, -1.0)


CHUNK = 256
GROUP = 2
MESH = pl.DeviceIdType.MESH


def kernel(line, u_ref, slot_ids, own_ids, res_ids, part_ids, out_ref,
           stream, part, row_best, res_best, part_best, own_best, message, returned, part_back, pair_back,
           out_send, swap_send, own_recv, part_send, part_recv, flow_send, ret_send, ret_recv,
           pb_send, pb_recv, pair_send, pair_recv, turn):
    rows = u_ref.shape[0]
    chunks = rows // CHUNK
    o, z = lax.axis_index("owner"), lax.axis_index("helper")
    middle = ((o + 1) // 2) % 2
    held = o + middle * (3 - 2 * o)
    sibling = o + 1 - 2 * (o % 2)
    near, outer = 1 + z // 2, 3 * (z // 2)
    is_middle, is_end = middle == 1, middle == 0
    is_inner, is_outer = z == near, z == outer
    takes = near == 1 + o % 2
    gives = near != 1 + o % 2

    barrier = pltpu.get_barrier_semaphore()

    def greet(owner, helper):
        pl.semaphore_signal(barrier, inc=1, device_id={"owner": owner, "helper": helper}, device_id_type=MESH)

    for step in range(1, line):
        greet(o, lax.rem(z + step, line))
    for helper in range(line):
        greet(sibling, jnp.int32(helper))

    @pl.when(is_middle)
    def _():
        for helper in range(line):
            greet(3 - o, jnp.int32(helper))
        pl.semaphore_wait(barrier, 3 * line - 1)

    @pl.when(is_end)
    def _():
        pl.semaphore_wait(barrier, 2 * line - 1)

    def piece(c):
        return pl.ds(pl.multiple_of(c * CHUNK, CHUNK), CHUNK)

    def remote(src, dst, send, recv, owner, helper):
        return pltpu.make_async_remote_copy(
            src_ref=src, dst_ref=dst, send_sem=send, recv_sem=recv,
            device_id={"owner": owner, "helper": helper}, device_id_type=MESH)

    def inward_end(c):
        return remote(u_ref.at[piece(c)], stream.at[outer, piece(c)], out_send.at[c], own_recv.at[outer, c], o, near)

    def inward_middle(c):
        return remote(u_ref.at[piece(c)], part.at[1, piece(c)], out_send.at[c], part_recv.at[1, c], o, near)

    def swap_near(c):
        return remote(u_ref.at[piece(c)], stream.at[near, piece(c)], swap_send.at[0, c], own_recv.at[near, c], 3 - o, near)

    def swap_outer(c):
        return remote(part.at[1, piece(c)], stream.at[outer, piece(c)], swap_send.at[1, c], own_recv.at[outer, c], 3 - o, near)

    def share_near(c):
        return remote(u_ref.at[piece(c)], part.at[0, piece(c)], part_send.at[0, c], part_recv.at[0, c], sibling, near)

    def share_outer(c):
        return remote(part.at[1, piece(c)], part.at[1, piece(c)], part_send.at[1, c], part_recv.at[1, c], sibling, near)

    def keep(c):
        return pltpu.make_async_copy(u_ref.at[piece(c)], stream.at[near, piece(c)], own_recv.at[near, c])

    def keep_part(c):
        return pltpu.make_async_copy(u_ref.at[piece(c)], part.at[0, piece(c)], part_recv.at[0, c])

    def flow(slot, c):
        return remote(stream.at[slot, piece(c)], stream.at[slot, piece(c)], flow_send.at[slot, c], own_recv.at[slot, c], o, 3 - near)

    def each_chunk(action):
        def step(c, carry):
            action(c)
            return carry

        lax.fori_loop(0, chunks, step, 0)

    def columns_loop(block, ids, columns_ref, column_ids, best, row_total, diagonal):
        def step(k, row_total):
            at = pl.ds(pl.multiple_of(k * CHUNK, CHUNK), CHUNK)
            scores = lax.dot_general(
                block, columns_ref[at, :], (((1,), (1,)), ((), ())), preferred_element_type=jnp.float32)
            same = ids == column_ids[:, at]
            if diagonal is not None:
                first = lax.broadcasted_iota(jnp.int32, scores.shape, 0) + diagonal * CHUNK
                second = lax.broadcasted_iota(jnp.int32, scores.shape, 1) + k * CHUNK
                same = same & (first != second)
            scores = jnp.where(same, scores, FLOOR)
            best[:, at] = jnp.maximum(best[:, at], jnp.max(scores.reshape(-1, 8, CHUNK), axis=0))
            if row_total is None:
                return None
            return jnp.maximum(row_total, jnp.maximum(scores[:, :128], scores[:, 128:]))

        return lax.fori_loop(0, rows // CHUNK, step, row_total, unroll=True)

    def slot_row(slot, c, size=CHUNK):
        return slot_ids[pl.ds(pl.multiple_of(slot * rows + c * size, size), size), :]

    def group(g):
        return pl.ds(pl.multiple_of(g * GROUP * CHUNK, GROUP * CHUNK), GROUP * CHUNK)

    def each_group(action):
        def step(g, carry):
            action(g)
            return carry

        lax.fori_loop(0, chunks // GROUP, step, 0)

    def in_group(g, action):
        for i in range(GROUP):
            action(g * GROUP + i)

    def self_chunk(c):
        columns_loop(u_ref[piece(c), :], slot_row(line, c), u_ref, own_ids, own_best, None, c)

    def with_res(slot, g, which):
        best = row_best.at[slot, group(g)]
        best[...] = columns_loop(
            stream[slot, group(g), :], slot_row(slot, g, GROUP * CHUNK), stream.at[near if which == 0 else outer],
            res_ids.at[which:which + 1], res_best.at[which], best[...], None)

    def with_part(slot, g, which):
        best = row_best.at[slot, group(g)]
        best[...] = columns_loop(
            stream[slot, group(g), :], slot_row(slot, g, GROUP * CHUNK), part.at[which],
            part_ids.at[which:which + 1], part_best.at[which], best[...], None)

    def folded(slot):
        return jnp.max(row_best[slot].T.reshape(16, 8, rows), axis=0)

    def to_home(slot):
        return remote(message.at[slot], returned.at[near - 1], ret_send.at[slot], ret_recv.at[near - 1], held, slot)

    def from_holder(which):
        return remote(message.at[z], returned.at[which], ret_send.at[z], ret_recv.at[which], held, near)

    def part_home(which):
        return remote(part_best.at[which], part_back, pb_send.at[which], pb_recv, sibling, near if which == 0 else outer)

    pair_home = remote(part_best.at[1], pair_back, pair_send, pair_recv, o, outer)
    there, there_outer = 3 - near, 3 - outer

    own_best[...] = jnp.full_like(own_best, FLOOR)

    @pl.when(is_outer)
    def _():
        @pl.when(is_middle)
        def _():
            each_chunk(lambda c: inward_middle(c).start())
            for c in range(chunks - 1):
                inward_middle(c).wait_send()
            pl.semaphore_signal(turn, inc=1, device_id={"owner": sibling, "helper": outer}, device_id_type=MESH)
            inward_middle(chunks - 1).wait_send()

        @pl.when(is_end)
        def _():
            pl.semaphore_wait(turn, 1)
            each_chunk(lambda c: inward_end(c).start())

        each_chunk(self_chunk)

    @pl.when(is_inner)
    def _():
        @pl.when(is_middle)
        def _():
            each_chunk(lambda c: swap_near(c).start())
            each_chunk(lambda c: share_near(c).start())

        @pl.when(is_end)
        def _():
            each_chunk(lambda c: keep(c).start())

        @pl.when(o == 2)
        def _():
            each_chunk(lambda c: keep_part(c).start())

        row_best[...] = jnp.full_like(row_best, FLOOR)
        res_best[...] = jnp.full_like(res_best, FLOOR)
        part_best[...] = jnp.full_like(part_best, FLOOR)

        def kept(c):
            keep(c).wait()

            @pl.when(gives)
            def _():
                flow(near, c).start()

        @pl.when(is_end)
        def _():
            each_chunk(kept)

            each_chunk(self_chunk)

        def first(c):
            swap_near(c).wait_recv()

            @pl.when(gives)
            def _():
                flow(near, c).start()

            inward_middle(c).wait_recv()
            swap_outer(c).start()
            share_outer(c).start()
            self_chunk(c)

        @pl.when(is_middle)
        def _():
            each_chunk(first)

        @pl.when(is_end)
        def _():
            each_chunk(lambda c: share_near(c).wait_recv())

        @pl.when(o == 2)
        def _():
            each_chunk(lambda c: keep_part(c).wait())

        @pl.when(o != 1)
        def _():
            each_group(lambda g: with_part(near, g, 0))

        @pl.when(is_end)
        def _():
            each_chunk(lambda c: share_outer(c).wait_recv())

        @pl.when(takes)
        def _():
            def early(g):
                in_group(g, lambda c: flow(there, c).wait_recv())
                with_res(there, g, 0)

                @pl.when(o != 1)
                def _():
                    with_part(near, g, 1)
                    for which in range(2):
                        with_part(there, g, which)

            each_group(early)

        def relay(c):
            @pl.when(is_middle)
            def _():
                swap_outer(c).wait_recv()

            @pl.when(is_end)
            def _():
                inward_end(c).wait_recv()

            @pl.when(gives)
            def _():
                flow(outer, c).start()

        def late(g):
            in_group(g, relay)
            with_res(outer, g, 0)

            @pl.when(o != 1)
            def _():
                with_part(outer, g, 1)

                @pl.when(gives)
                def _():
                    with_part(outer, g, 0)

        each_group(late)

        @pl.when(takes)
        def _():
            each_group(lambda g: with_res(there, g, 1))
            message[there] = folded(there)
            to_home(there).start()

            def last(g):
                in_group(g, lambda c: flow(there_outer, c).wait_recv())
                for which in range(2):
                    with_res(there_outer, g, which)

                @pl.when(o != 1)
                def _():
                    for which in range(2):
                        with_part(there_outer, g, which)

            each_group(last)
            message[there_outer] = folded(there_outer)
            to_home(there_outer).start()

        message[outer] = jnp.maximum(folded(outer), res_best[1])
        to_home(outer).start()
        message[near] = jnp.maximum(folded(near), res_best[0])

        @pl.when(is_middle)
        def _():
            to_home(near).start()

        @pl.when(is_end)
        def _():
            part_home(0).start()
            part_home(1).start()
            own_best[...] = jnp.maximum(own_best[...], message[near])

        @pl.when(o == 2)
        def _():
            pair_home.start()
            own_best[...] = jnp.maximum(own_best[...], part_best[0])

    @pl.when(is_outer | is_middle)
    def _():
        from_holder(near - 1).wait_recv()
        own_best[...] = jnp.maximum(own_best[...], returned[near - 1])

    @pl.when(near != 1 + held % 2)
    def _():
        from_holder(2 - near).wait_recv()
        own_best[...] = jnp.maximum(own_best[...], returned[2 - near])

    @pl.when(is_middle)
    def _():
        part_home(0).wait_recv()
        own_best[...] = jnp.maximum(own_best[...], part_back[...])

    @pl.when((o == 2) & is_outer)
    def _():
        pair_home.wait_recv()
        own_best[...] = jnp.maximum(own_best[...], pair_back[...])

    out_ref[...] = jnp.maximum(jnp.max(own_best[...], axis=0, keepdims=True), -1.0)

    @pl.when(is_outer & is_end)
    def _():
        each_chunk(lambda c: inward_end(c).wait_send())

    @pl.when(is_inner)
    def _():
        to_home(outer).wait_send()

        @pl.when(takes)
        def _():
            to_home(there).wait_send()
            to_home(there_outer).wait_send()

        @pl.when(gives)
        def _():
            each_chunk(lambda c: flow(near, c).wait_send())
            each_chunk(lambda c: flow(outer, c).wait_send())

        @pl.when(is_middle)
        def _():
            to_home(near).wait_send()
            for copy in (swap_near, swap_outer, share_near, share_outer):
                each_chunk(lambda c, copy=copy: copy(c).wait_send())

        @pl.when(is_end)
        def _():
            part_home(0).wait_send()
            part_home(1).wait_send()

        @pl.when(o == 2)
        def _():
            pair_home.wait_send()


def chain_body(line, embeddings, cluster_sizes):
    unit_rows = normalize(embeddings)
    rows, width = unit_rows.shape
    ends = jnp.cumsum(cluster_sizes)
    o, z = lax.axis_index("owner"), lax.axis_index("helper")
    held = jnp.where((o == 1) | (o == 2), 3 - o, o)
    ids = lambda block, total: cluster_of(block * rows, total, ends)
    own_ids = ids(o * line + z, rows)
    slot_ids = jnp.concatenate([ids(held * line, rows * line), own_ids])[:, None]
    near, outer = 1 + z // 2, 3 * (z // 2)
    shared = jnp.where(o == 0, 1, 2) * line
    res_ids = jnp.stack([ids(held * line + near, rows), ids(held * line + outer, rows)])
    part_ids = jnp.stack([ids(shared + near, rows), ids(shared + outer, rows)])
    chunks = rows // CHUNK
    best = pl.pallas_call(
        functools.partial(kernel, line),
        out_shape=jax.ShapeDtypeStruct((1, rows), jnp.float32),
        in_specs=[pl.BlockSpec(memory_space=pltpu.VMEM)] * 5,
        out_specs=pl.BlockSpec(memory_space=pltpu.VMEM),
        scratch_shapes=[
            pltpu.VMEM((line, rows, width), jnp.bfloat16),
            pltpu.VMEM((2, rows, width), jnp.bfloat16),
            pltpu.VMEM((line, rows, 128), jnp.float32),
            pltpu.VMEM((2, 8, rows), jnp.float32),
            pltpu.VMEM((2, 8, rows), jnp.float32),
            pltpu.VMEM((8, rows), jnp.float32),
            pltpu.VMEM((line, 8, rows), jnp.float32),
            pltpu.VMEM((2, 8, rows), jnp.float32),
            pltpu.VMEM((8, rows), jnp.float32),
            pltpu.VMEM((8, rows), jnp.float32),
            pltpu.SemaphoreType.DMA((chunks,)),
            pltpu.SemaphoreType.DMA((2, chunks)),
            pltpu.SemaphoreType.DMA((line, chunks)),
            pltpu.SemaphoreType.DMA((2, chunks)),
            pltpu.SemaphoreType.DMA((2, chunks)),
            pltpu.SemaphoreType.DMA((line, chunks)),
            pltpu.SemaphoreType.DMA((line,)),
            pltpu.SemaphoreType.DMA((2,)),
            pltpu.SemaphoreType.DMA((2,)),
            pltpu.SemaphoreType.DMA,
            pltpu.SemaphoreType.DMA,
            pltpu.SemaphoreType.DMA,
            pltpu.SemaphoreType.REGULAR,
        ],
        compiler_params=pltpu.CompilerParams(
            collective_id=0, has_side_effects=True, vmem_limit_bytes=48 * 2**20
        ),
    )(unit_rows, slot_ids, own_ids[None], res_ids, part_ids)
    return best.reshape(rows)


def solution(mesh):
    placed = (P(("parts", "owner", "helper"), None), P("parts"))
    line = mesh.shape["helper"]
    chained = mesh.shape["owner"] == 4 and line == REACH
    return jax.shard_map(
        functools.partial(chain_body, line) if chained else body,
        mesh=mesh, in_specs=placed, out_specs=P(("parts", "owner", "helper")), check_vma=False
    )
```

```python
import functools
import math

import jax
import jax.numpy as jnp
from jax import lax
from jax.experimental import pallas as pl
from jax.experimental.pallas import tpu as pltpu
from jax.sharding import PartitionSpec as P

REACH = 4


FLOOR = -2.0


def from_behind(value, axis, steps):
    count = lax.axis_size(axis)
    initial, last = (max(0, -steps), min(count, count - steps))
    return lax.ppermute(value, axis, [(source, source + steps) for source in range(initial, last)])


def normalize(embeddings):
    values = embeddings.astype(jnp.float32)
    factor = lax.rsqrt(jnp.mean(values * values, axis=1, keepdims=True) + 1e-06) * (
        1.0 / math.sqrt(values.shape[1])
    )
    return (values * factor).astype(jnp.bfloat16)


def cluster_of(first_row, row_total, cluster_ends):
    positions = first_row + jnp.arange(row_total, dtype=jnp.int32)
    located = jnp.sum((positions[:, None] >= cluster_ends[None, :]).astype(jnp.int32), axis=1)
    return jnp.where(positions < 0, -1, located)


def tile_best(row_unit, row_cluster, column_unit, column_cluster, skip_self):
    scores = lax.dot_general(
        row_unit, column_unit, (((1,), (1,)), ((), ())), preferred_element_type=jnp.float32
    )
    same_cluster = row_cluster[:, None] == column_cluster[None, :]
    if skip_self:
        row_total = row_unit.shape[0]
        same_cluster = same_cluster & (
            lax.broadcasted_iota(jnp.int32, (row_total, row_total), 0)
            != lax.broadcasted_iota(jnp.int32, (row_total, row_total), 1)
        )
    masked = jnp.where(same_cluster, scores, FLOOR)
    return (jnp.max(masked, axis=1), jnp.max(masked, axis=0))


def intersections(row_cluster, column_cluster):
    return (row_cluster[0] <= column_cluster[-1]) & (column_cluster[0] <= row_cluster[-1])


def body(embeddings, cluster_sizes):
    unit_rows = normalize(embeddings)
    row_total = unit_rows.shape[0]
    cluster_ends = jnp.cumsum(cluster_sizes)
    device_index = lax.axis_index(("owner", "helper"))
    first_row = device_index * row_total
    own_cluster = cluster_of(first_row, row_total, cluster_ends)
    best_score, unused = tile_best(unit_rows, own_cluster, unit_rows, own_cluster, True)
    blank = jnp.full((row_total,), FLOOR, jnp.float32)
    for offset in range(1, REACH + 1):
        lower_rows = from_behind(unit_rows, ("owner", "helper"), offset)
        lower_cluster = cluster_of(first_row - offset * row_total, row_total, cluster_ends)
        lower_best = lax.cond(
            intersections(own_cluster, lower_cluster),
            lambda: tile_best(unit_rows, own_cluster, lower_rows, lower_cluster, False)[0],
            lambda: blank,
        )
        best_score = jnp.maximum(best_score, lower_best)
        upper_rows = from_behind(unit_rows, ("owner", "helper"), -offset)
        upper_cluster = cluster_of(first_row + offset * row_total, row_total, cluster_ends)
        upper_best = lax.cond(
            intersections(own_cluster, upper_cluster),
            lambda: tile_best(unit_rows, own_cluster, upper_rows, upper_cluster, False)[0],
            lambda: blank,
        )
        best_score = jnp.maximum(best_score, upper_best)
    return jnp.maximum(best_score, -1.0)


CHUNK = 256
GROUP = 2
MESH = pl.DeviceIdType.MESH


def kernel(line, raw_ref, ends_row, ends_column, out_ref, u_ref, slot_ids, own_ids, res_ids, part_ids,
           stream, part, row_best, res_best, part_best, own_best, message, returned, part_back, pair_back,
           out_send, swap_send, own_recv, part_send, part_recv, flow_send, ret_send, ret_recv,
           pb_send, pb_recv, pair_send, pair_recv, turn):
    rows = u_ref.shape[0]
    chunks = rows // CHUNK
    o, z = lax.axis_index("owner"), lax.axis_index("helper")
    middle = ((o + 1) // 2) % 2
    held = o + middle * (3 - 2 * o)
    sibling = o + 1 - 2 * (o % 2)
    near, outer = 1 + z // 2, 3 * (z // 2)
    is_middle, is_end = middle == 1, middle == 0
    is_inner, is_outer = z == near, z == outer
    takes = near == 1 + o % 2
    gives = near != 1 + o % 2

    barrier = pltpu.get_barrier_semaphore()

    def greet(owner, helper):
        pl.semaphore_signal(barrier, inc=1, device_id={"owner": owner, "helper": helper}, device_id_type=MESH)

    for step in range(1, line):
        greet(o, lax.rem(z + step, line))
    for helper in range(line):
        greet(sibling, jnp.int32(helper))

    @pl.when(is_middle)
    def _():
        for helper in range(line):
            greet(3 - o, jnp.int32(helper))

    def unit_step(c, carry):
        at = pl.ds(pl.multiple_of(c * CHUNK, CHUNK), CHUNK)
        u_ref[at, :] = normalize(raw_ref[at, :])
        return carry

    lax.fori_loop(0, chunks, unit_step, 0)

    @pl.when(is_middle)
    def _():
        pl.semaphore_wait(barrier, 3 * line - 1)

    @pl.when(is_end)
    def _():
        pl.semaphore_wait(barrier, 2 * line - 1)

    def piece(c):
        return pl.ds(pl.multiple_of(c * CHUNK, CHUNK), CHUNK)

    def remote(src, dst, send, recv, owner, helper):
        return pltpu.make_async_remote_copy(
            src_ref=src, dst_ref=dst, send_sem=send, recv_sem=recv,
            device_id={"owner": owner, "helper": helper}, device_id_type=MESH)

    def inward_end(c):
        return remote(u_ref.at[piece(c)], stream.at[outer, piece(c)], out_send.at[c], own_recv.at[outer, c], o, near)

    def inward_middle(c):
        return remote(u_ref.at[piece(c)], part.at[1, piece(c)], out_send.at[c], part_recv.at[1, c], o, near)

    def swap_near(c):
        return remote(u_ref.at[piece(c)], stream.at[near, piece(c)], swap_send.at[0, c], own_recv.at[near, c], 3 - o, near)

    def swap_outer(c):
        return remote(part.at[1, piece(c)], stream.at[outer, piece(c)], swap_send.at[1, c], own_recv.at[outer, c], 3 - o, near)

    def share_near(c):
        return remote(u_ref.at[piece(c)], part.at[0, piece(c)], part_send.at[0, c], part_recv.at[0, c], sibling, near)

    def share_outer(c):
        return remote(part.at[1, piece(c)], part.at[1, piece(c)], part_send.at[1, c], part_recv.at[1, c], sibling, near)

    def keep(c):
        return pltpu.make_async_copy(u_ref.at[piece(c)], stream.at[near, piece(c)], own_recv.at[near, c])

    def keep_part(c):
        return pltpu.make_async_copy(u_ref.at[piece(c)], part.at[0, piece(c)], part_recv.at[0, c])

    def flow(slot, c):
        return remote(stream.at[slot, piece(c)], stream.at[slot, piece(c)], flow_send.at[slot, c], own_recv.at[slot, c], o, 3 - near)

    def each_chunk(action):
        def step(c, carry):
            action(c)
            return carry

        lax.fori_loop(0, chunks, step, 0)

    def columns_loop(block, ids, columns_ref, column_ids, best, row_total, diagonal):
        def step(k, row_total):
            at = pl.ds(pl.multiple_of(k * CHUNK, CHUNK), CHUNK)
            scores = lax.dot_general(
                block, columns_ref[at, :], (((1,), (1,)), ((), ())), preferred_element_type=jnp.float32)
            same = ids == column_ids[:, at]
            if diagonal is not None:
                first = lax.broadcasted_iota(jnp.int32, scores.shape, 0) + diagonal * CHUNK
                second = lax.broadcasted_iota(jnp.int32, scores.shape, 1) + k * CHUNK
                same = same & (first != second)
            scores = jnp.where(same, scores, FLOOR)
            best[:, at] = jnp.maximum(best[:, at], jnp.max(scores.reshape(-1, 8, CHUNK), axis=0))
            if row_total is None:
                return None
            return jnp.maximum(row_total, jnp.maximum(scores[:, :128], scores[:, 128:]))

        return lax.fori_loop(0, rows // CHUNK, step, row_total, unroll=True)

    def slot_row(slot, c, size=CHUNK):
        return slot_ids[pl.ds(pl.multiple_of(slot * rows + c * size, size), size), :]

    def group(g):
        return pl.ds(pl.multiple_of(g * GROUP * CHUNK, GROUP * CHUNK), GROUP * CHUNK)

    def each_group(action):
        def step(g, carry):
            action(g)
            return carry

        lax.fori_loop(0, chunks // GROUP, step, 0)

    def in_group(g, action):
        for i in range(GROUP):
            action(g * GROUP + i)

    def self_chunk(c):
        columns_loop(u_ref[piece(c), :], slot_row(line, c), u_ref, own_ids, own_best, None, c)

    def with_res(slot, g, which):
        best = row_best.at[slot, group(g)]
        best[...] = columns_loop(
            stream[slot, group(g), :], slot_row(slot, g, GROUP * CHUNK), stream.at[near if which == 0 else outer],
            res_ids.at[which:which + 1], res_best.at[which], best[...], None)

    def with_part(slot, g, which):
        best = row_best.at[slot, group(g)]
        best[...] = columns_loop(
            stream[slot, group(g), :], slot_row(slot, g, GROUP * CHUNK), part.at[which],
            part_ids.at[which:which + 1], part_best.at[which], best[...], None)

    def folded(slot):
        return jnp.max(row_best[slot].T.reshape(16, 8, rows), axis=0)

    def to_home(slot):
        return remote(message.at[slot], returned.at[near - 1], ret_send.at[slot], ret_recv.at[near - 1], held, slot)

    def from_holder(which):
        return remote(message.at[z], returned.at[which], ret_send.at[z], ret_recv.at[which], held, near)

    def part_home(which):
        return remote(part_best.at[which], part_back, pb_send.at[which], pb_recv, sibling, near if which == 0 else outer)

    pair_home = remote(part_best.at[1], pair_back, pair_send, pair_recv, o, outer)
    there, there_outer = 3 - near, 3 - outer

    own_best[...] = jnp.full_like(own_best, FLOOR)

    def located(block):
        shape = (ends_column.shape[0], rows)
        position = block * rows + lax.broadcasted_iota(jnp.int32, shape, 1)
        return jnp.sum(jnp.where(position >= ends_column[...], 1.0, 0.0), axis=0, keepdims=True)

    def locate_rows(first, block):
        def step(c, carry):
            shape = (CHUNK, ends_row.shape[1])
            position = block * rows + c * CHUNK + lax.broadcasted_iota(jnp.int32, shape, 0)
            at = pl.ds(pl.multiple_of(first * rows + c * CHUNK, CHUNK), CHUNK)
            slot_ids[at, :] = jnp.sum(jnp.where(position >= ends_row[...], 1.0, 0.0), axis=1, keepdims=True)
            return carry

        lax.fori_loop(0, chunks, step, 0)

    def locate():
        own_ids[...] = located(o * line + z)
        locate_rows(line, o * line + z)

    @pl.when(is_outer)
    def _():
        @pl.when(is_middle)
        def _():
            each_chunk(lambda c: inward_middle(c).start())
            locate()
            for c in range(chunks - 1):
                inward_middle(c).wait_send()
            pl.semaphore_signal(turn, inc=1, device_id={"owner": sibling, "helper": outer}, device_id_type=MESH)
            inward_middle(chunks - 1).wait_send()

        @pl.when(is_end)
        def _():
            locate()
            pl.semaphore_wait(turn, 1)
            each_chunk(lambda c: inward_end(c).start())

        each_chunk(self_chunk)

    @pl.when(is_inner)
    def _():
        @pl.when(is_middle)
        def _():
            each_chunk(lambda c: swap_near(c).start())
            each_chunk(lambda c: share_near(c).start())

        @pl.when(is_end)
        def _():
            each_chunk(lambda c: keep(c).start())

        @pl.when(o == 2)
        def _():
            each_chunk(lambda c: keep_part(c).start())

        row_best[...] = jnp.full_like(row_best, FLOOR)
        res_best[...] = jnp.full_like(res_best, FLOOR)
        part_best[...] = jnp.full_like(part_best, FLOOR)

        def locate_all():
            locate()
            res_ids[0:1, :] = located(held * line + near)
            res_ids[1:2, :] = located(held * line + outer)
            shared = (1 + jnp.minimum(o, 1)) * line
            part_ids[0:1, :] = located(shared + near)
            part_ids[1:2, :] = located(shared + outer)
            for slot in range(line):
                locate_rows(slot, held * line + slot)

        def kept(c):
            keep(c).wait()

            @pl.when(gives)
            def _():
                flow(near, c).start()

        @pl.when(is_end)
        def _():
            each_chunk(kept)
            locate_all()
            each_chunk(self_chunk)

        def first(c):
            swap_near(c).wait_recv()

            @pl.when(gives)
            def _():
                flow(near, c).start()

            inward_middle(c).wait_recv()
            swap_outer(c).start()
            share_outer(c).start()
            self_chunk(c)

        @pl.when(is_middle)
        def _():
            locate_all()
            each_chunk(first)

        @pl.when(is_end)
        def _():
            each_chunk(lambda c: share_near(c).wait_recv())

        @pl.when(o == 2)
        def _():
            each_chunk(lambda c: keep_part(c).wait())

        @pl.when(o != 1)
        def _():
            each_group(lambda g: with_part(near, g, 0))

        @pl.when(is_end)
        def _():
            each_chunk(lambda c: share_outer(c).wait_recv())

        @pl.when(takes)
        def _():
            def early(g):
                in_group(g, lambda c: flow(there, c).wait_recv())
                with_res(there, g, 0)

                @pl.when(o != 1)
                def _():
                    with_part(near, g, 1)
                    for which in range(2):
                        with_part(there, g, which)

            each_group(early)

        def relay(c):
            @pl.when(is_middle)
            def _():
                swap_outer(c).wait_recv()

            @pl.when(is_end)
            def _():
                inward_end(c).wait_recv()

            @pl.when(gives)
            def _():
                flow(outer, c).start()

        def late(g):
            in_group(g, relay)
            with_res(outer, g, 0)

            @pl.when(o != 1)
            def _():
                with_part(outer, g, 1)

                @pl.when(gives)
                def _():
                    with_part(outer, g, 0)

        each_group(late)

        @pl.when(takes)
        def _():
            each_group(lambda g: with_res(there, g, 1))
            message[there] = folded(there)
            to_home(there).start()

            def last(g):
                in_group(g, lambda c: flow(there_outer, c).wait_recv())
                for which in range(2):
                    with_res(there_outer, g, which)

                @pl.when(o != 1)
                def _():
                    for which in range(2):
                        with_part(there_outer, g, which)

            each_group(last)
            message[there_outer] = folded(there_outer)
            to_home(there_outer).start()

        message[outer] = jnp.maximum(folded(outer), res_best[1])
        to_home(outer).start()
        message[near] = jnp.maximum(folded(near), res_best[0])

        @pl.when(is_middle)
        def _():
            to_home(near).start()

        @pl.when(is_end)
        def _():
            part_home(0).start()
            part_home(1).start()
            own_best[...] = jnp.maximum(own_best[...], message[near])

        @pl.when(o == 2)
        def _():
            pair_home.start()
            own_best[...] = jnp.maximum(own_best[...], part_best[0])

    @pl.when(is_outer | is_middle)
    def _():
        from_holder(near - 1).wait_recv()
        own_best[...] = jnp.maximum(own_best[...], returned[near - 1])

    @pl.when(near != 1 + held % 2)
    def _():
        from_holder(2 - near).wait_recv()
        own_best[...] = jnp.maximum(own_best[...], returned[2 - near])

    @pl.when(is_middle)
    def _():
        part_home(0).wait_recv()
        own_best[...] = jnp.maximum(own_best[...], part_back[...])

    @pl.when((o == 2) & is_outer)
    def _():
        pair_home.wait_recv()
        own_best[...] = jnp.maximum(own_best[...], pair_back[...])

    out_ref[...] = jnp.maximum(jnp.max(own_best[...], axis=0, keepdims=True), -1.0)

    @pl.when(is_outer & is_end)
    def _():
        each_chunk(lambda c: inward_end(c).wait_send())

    @pl.when(is_inner)
    def _():
        to_home(outer).wait_send()

        @pl.when(takes)
        def _():
            to_home(there).wait_send()
            to_home(there_outer).wait_send()

        @pl.when(gives)
        def _():
            each_chunk(lambda c: flow(near, c).wait_send())
            each_chunk(lambda c: flow(outer, c).wait_send())

        @pl.when(is_middle)
        def _():
            to_home(near).wait_send()
            for copy in (swap_near, swap_outer, share_near, share_outer):
                each_chunk(lambda c, copy=copy: copy(c).wait_send())

        @pl.when(is_end)
        def _():
            part_home(0).wait_send()
            part_home(1).wait_send()

        @pl.when(o == 2)
        def _():
            pair_home.wait_send()


def chain_body(line, embeddings, cluster_sizes):
    rows, width = embeddings.shape
    ends = jnp.cumsum(cluster_sizes)
    chunks = rows // CHUNK
    best = pl.pallas_call(
        functools.partial(kernel, line),
        out_shape=jax.ShapeDtypeStruct((1, rows), jnp.float32),
        in_specs=[pl.BlockSpec(memory_space=pltpu.VMEM)] * 3,
        out_specs=pl.BlockSpec(memory_space=pltpu.VMEM),
        scratch_shapes=[
            pltpu.VMEM((rows, width), jnp.bfloat16),
            pltpu.VMEM(((line + 1) * rows, 1), jnp.float32),
            pltpu.VMEM((1, rows), jnp.float32),
            pltpu.VMEM((2, rows), jnp.float32),
            pltpu.VMEM((2, rows), jnp.float32),
            pltpu.VMEM((line, rows, width), jnp.bfloat16),
            pltpu.VMEM((2, rows, width), jnp.bfloat16),
            pltpu.VMEM((line, rows, 128), jnp.float32),
            pltpu.VMEM((2, 8, rows), jnp.float32),
            pltpu.VMEM((2, 8, rows), jnp.float32),
            pltpu.VMEM((8, rows), jnp.float32),
            pltpu.VMEM((line, 8, rows), jnp.float32),
            pltpu.VMEM((2, 8, rows), jnp.float32),
            pltpu.VMEM((8, rows), jnp.float32),
            pltpu.VMEM((8, rows), jnp.float32),
            pltpu.SemaphoreType.DMA((chunks,)),
            pltpu.SemaphoreType.DMA((2, chunks)),
            pltpu.SemaphoreType.DMA((line, chunks)),
            pltpu.SemaphoreType.DMA((2, chunks)),
            pltpu.SemaphoreType.DMA((2, chunks)),
            pltpu.SemaphoreType.DMA((line, chunks)),
            pltpu.SemaphoreType.DMA((line,)),
            pltpu.SemaphoreType.DMA((2,)),
            pltpu.SemaphoreType.DMA((2,)),
            pltpu.SemaphoreType.DMA,
            pltpu.SemaphoreType.DMA,
            pltpu.SemaphoreType.DMA,
            pltpu.SemaphoreType.REGULAR,
        ],
        compiler_params=pltpu.CompilerParams(
            collective_id=0, has_side_effects=True, vmem_limit_bytes=48 * 2**20
        ),
    )(embeddings, ends[None], ends[:, None])
    return best.reshape(rows)


def solution(mesh):
    placed = (P(("parts", "owner", "helper"), None), P("parts"))
    line = mesh.shape["helper"]
    chained = mesh.shape["owner"] == 4 and line == REACH
    return jax.shard_map(
        functools.partial(chain_body, line) if chained else body,
        mesh=mesh, in_specs=placed, out_specs=P(("parts", "owner", "helper")), check_vma=False
    )
```

```python
import functools
import math

import jax
import jax.numpy as jnp
from jax import lax
from jax.experimental import pallas as pl
from jax.experimental.pallas import tpu as pltpu
from jax.sharding import PartitionSpec as P

REACH = 4


FLOOR = -2.0


def from_behind(value, axis, steps):
    count = lax.axis_size(axis)
    initial, last = (max(0, -steps), min(count, count - steps))
    return lax.ppermute(value, axis, [(source, source + steps) for source in range(initial, last)])


def normalize(embeddings):
    values = embeddings.astype(jnp.float32)
    factor = lax.rsqrt(jnp.mean(values * values, axis=1, keepdims=True) + 1e-06) * (
        1.0 / math.sqrt(values.shape[1])
    )
    return (values * factor).astype(jnp.bfloat16)


def cluster_of(first_row, row_total, cluster_ends):
    positions = first_row + jnp.arange(row_total, dtype=jnp.int32)
    located = jnp.sum((positions[:, None] >= cluster_ends[None, :]).astype(jnp.int32), axis=1)
    return jnp.where(positions < 0, -1, located)


def tile_best(row_unit, row_cluster, column_unit, column_cluster, skip_self):
    scores = lax.dot_general(
        row_unit, column_unit, (((1,), (1,)), ((), ())), preferred_element_type=jnp.float32
    )
    same_cluster = row_cluster[:, None] == column_cluster[None, :]
    if skip_self:
        row_total = row_unit.shape[0]
        same_cluster = same_cluster & (
            lax.broadcasted_iota(jnp.int32, (row_total, row_total), 0)
            != lax.broadcasted_iota(jnp.int32, (row_total, row_total), 1)
        )
    masked = jnp.where(same_cluster, scores, FLOOR)
    return (jnp.max(masked, axis=1), jnp.max(masked, axis=0))


def intersections(row_cluster, column_cluster):
    return (row_cluster[0] <= column_cluster[-1]) & (column_cluster[0] <= row_cluster[-1])


def body(embeddings, cluster_sizes):
    unit_rows = normalize(embeddings)
    row_total = unit_rows.shape[0]
    cluster_ends = jnp.cumsum(cluster_sizes)
    device_index = lax.axis_index(("owner", "helper"))
    first_row = device_index * row_total
    own_cluster = cluster_of(first_row, row_total, cluster_ends)
    best_score, unused = tile_best(unit_rows, own_cluster, unit_rows, own_cluster, True)
    blank = jnp.full((row_total,), FLOOR, jnp.float32)
    for offset in range(1, REACH + 1):
        lower_rows = from_behind(unit_rows, ("owner", "helper"), offset)
        lower_cluster = cluster_of(first_row - offset * row_total, row_total, cluster_ends)
        lower_best = lax.cond(
            intersections(own_cluster, lower_cluster),
            lambda: tile_best(unit_rows, own_cluster, lower_rows, lower_cluster, False)[0],
            lambda: blank,
        )
        best_score = jnp.maximum(best_score, lower_best)
        upper_rows = from_behind(unit_rows, ("owner", "helper"), -offset)
        upper_cluster = cluster_of(first_row + offset * row_total, row_total, cluster_ends)
        upper_best = lax.cond(
            intersections(own_cluster, upper_cluster),
            lambda: tile_best(unit_rows, own_cluster, upper_rows, upper_cluster, False)[0],
            lambda: blank,
        )
        best_score = jnp.maximum(best_score, upper_best)
    return jnp.maximum(best_score, -1.0)


CHUNK = 256
GROUP = 2
MESH = pl.DeviceIdType.MESH


def kernel(line, raw_ref, ends_row, ends_column, out_ref, u_ref, slot_ids, own_ids, res_ids, part_ids,
           stream, part, row_best, res_best, part_best, own_best, message, returned, part_back, pair_back,
           out_send, swap_send, own_recv, part_send, part_recv, flow_send, ret_send, ret_recv,
           pb_send, pb_recv, pair_send, pair_recv, turn):
    rows = u_ref.shape[0]
    chunks = rows // CHUNK
    o, z = lax.axis_index("owner"), lax.axis_index("helper")
    middle = ((o + 1) // 2) % 2
    held = o + middle * (3 - 2 * o)
    sibling = o + 1 - 2 * (o % 2)
    near, outer = 1 + z // 2, 3 * (z // 2)
    is_middle, is_end = middle == 1, middle == 0
    is_inner, is_outer = z == near, z == outer
    takes = near == 1 + o % 2
    gives = near != 1 + o % 2

    barrier = pltpu.get_barrier_semaphore()

    def greet(owner, helper):
        pl.semaphore_signal(barrier, inc=1, device_id={"owner": owner, "helper": helper}, device_id_type=MESH)

    for step in range(1, line):
        greet(o, lax.rem(z + step, line))
    for helper in range(line):
        greet(sibling, jnp.int32(helper))

    @pl.when(is_middle)
    def _():
        for helper in range(line):
            greet(3 - o, jnp.int32(helper))

    def unit_step(c, carry):
        at = pl.ds(pl.multiple_of(c * CHUNK, CHUNK), CHUNK)
        u_ref[at, :] = normalize(raw_ref[at, :])
        return carry

    lax.fori_loop(0, chunks, unit_step, 0)

    @pl.when(is_middle)
    def _():
        pl.semaphore_wait(barrier, 3 * line - 1)

    @pl.when(is_end)
    def _():
        pl.semaphore_wait(barrier, 2 * line - 1)

    def piece(c):
        return pl.ds(pl.multiple_of(c * CHUNK, CHUNK), CHUNK)

    def remote(src, dst, send, recv, owner, helper):
        return pltpu.make_async_remote_copy(
            src_ref=src, dst_ref=dst, send_sem=send, recv_sem=recv,
            device_id={"owner": owner, "helper": helper}, device_id_type=MESH)

    def inward_end(c):
        return remote(u_ref.at[piece(c)], stream.at[outer, piece(c)], out_send.at[c], own_recv.at[outer, c], o, near)

    def inward_middle(c):
        return remote(u_ref.at[piece(c)], part.at[1, piece(c)], out_send.at[c], part_recv.at[1, c], o, near)

    def swap_near(c):
        return remote(u_ref.at[piece(c)], stream.at[near, piece(c)], swap_send.at[0, c], own_recv.at[near, c], 3 - o, near)

    def swap_outer(c):
        return remote(part.at[1, piece(c)], stream.at[outer, piece(c)], swap_send.at[1, c], own_recv.at[outer, c], 3 - o, near)

    def share_near(c):
        return remote(u_ref.at[piece(c)], part.at[0, piece(c)], part_send.at[0, c], part_recv.at[0, c], sibling, near)

    def share_outer(c):
        return remote(part.at[1, piece(c)], part.at[1, piece(c)], part_send.at[1, c], part_recv.at[1, c], sibling, near)

    def keep(c):
        return pltpu.make_async_copy(u_ref.at[piece(c)], stream.at[near, piece(c)], own_recv.at[near, c])

    def keep_part(c):
        return pltpu.make_async_copy(u_ref.at[piece(c)], part.at[0, piece(c)], part_recv.at[0, c])

    def flow(slot, c):
        return remote(stream.at[slot, piece(c)], stream.at[slot, piece(c)], flow_send.at[slot, c], own_recv.at[slot, c], o, 3 - near)

    def each_chunk(action):
        def step(c, carry):
            action(c)
            return carry

        lax.fori_loop(0, chunks, step, 0)

    def columns_loop(block, ids, columns_ref, column_ids, best, row_total, diagonal):
        def step(k, row_total):
            at = pl.ds(pl.multiple_of(k * CHUNK, CHUNK), CHUNK)
            scores = lax.dot_general(
                block, columns_ref[at, :], (((1,), (1,)), ((), ())), preferred_element_type=jnp.float32)
            same = ids == column_ids[:, at]
            if diagonal is not None:
                first = lax.broadcasted_iota(jnp.int32, scores.shape, 0) + diagonal * CHUNK
                second = lax.broadcasted_iota(jnp.int32, scores.shape, 1) + k * CHUNK
                same = same & (first != second)
            scores = jnp.where(same, scores, FLOOR)
            best[:, at] = jnp.maximum(best[:, at], jnp.max(scores.reshape(-1, 8, CHUNK), axis=0))
            if row_total is None:
                return None
            return jnp.maximum(row_total, jnp.maximum(scores[:, :128], scores[:, 128:]))

        return lax.fori_loop(0, rows // CHUNK, step, row_total, unroll=True)

    def slot_row(slot, c, size=CHUNK):
        return slot_ids[pl.ds(pl.multiple_of(slot * rows + c * size, size), size), :]

    def group(g):
        return pl.ds(pl.multiple_of(g * GROUP * CHUNK, GROUP * CHUNK), GROUP * CHUNK)

    def each_group(action):
        def step(g, carry):
            action(g)
            return carry

        lax.fori_loop(0, chunks // GROUP, step, 0)

    def in_group(g, action):
        for i in range(GROUP):
            action(g * GROUP + i)

    def self_chunk(c):
        columns_loop(u_ref[piece(c), :], slot_row(line, c), u_ref, own_ids, own_best, None, c)

    def with_res(slot, g, which):
        best = row_best.at[slot, group(g)]
        best[...] = columns_loop(
            stream[slot, group(g), :], slot_row(slot, g, GROUP * CHUNK), stream.at[near if which == 0 else outer],
            res_ids.at[which:which + 1], res_best.at[which], best[...], None)

    def with_part(slot, g, which):
        best = row_best.at[slot, group(g)]
        best[...] = columns_loop(
            stream[slot, group(g), :], slot_row(slot, g, GROUP * CHUNK), part.at[which],
            part_ids.at[which:which + 1], part_best.at[which], best[...], None)

    def folded(slot):
        return jnp.max(row_best[slot].T.reshape(16, 8, rows), axis=0)

    def to_home(slot):
        return remote(message.at[slot], returned.at[near - 1], ret_send.at[slot], ret_recv.at[near - 1], held, slot)

    def from_holder(which):
        return remote(message.at[z], returned.at[which], ret_send.at[z], ret_recv.at[which], held, near)

    def part_home(which):
        return remote(part_best.at[which], part_back, pb_send.at[which], pb_recv, sibling, near if which == 0 else outer)

    pair_home = remote(part_best.at[1], pair_back, pair_send, pair_recv, o, outer)
    there, there_outer = 3 - near, 3 - outer

    own_best[...] = jnp.full_like(own_best, FLOOR)

    def located(block):
        shape = (ends_column.shape[0], rows)
        position = block * rows + lax.broadcasted_iota(jnp.int32, shape, 1)
        return jnp.sum(jnp.where(position >= ends_column[...], 1.0, 0.0), axis=0, keepdims=True)

    def locate_rows(first, block):
        def step(c, carry):
            shape = (CHUNK, ends_row.shape[1])
            position = block * rows + c * CHUNK + lax.broadcasted_iota(jnp.int32, shape, 0)
            at = pl.ds(pl.multiple_of(first * rows + c * CHUNK, CHUNK), CHUNK)
            slot_ids[at, :] = jnp.sum(jnp.where(position >= ends_row[...], 1.0, 0.0), axis=1, keepdims=True)
            return carry

        lax.fori_loop(0, chunks, step, 0)

    def locate():
        own_ids[...] = located(o * line + z)
        locate_rows(line, o * line + z)

    @pl.when(is_outer)
    def _():
        @pl.when(is_middle)
        def _():
            each_chunk(lambda c: inward_middle(c).start())
            locate()
            for c in range(chunks - 1):
                inward_middle(c).wait_send()
            pl.semaphore_signal(turn, inc=1, device_id={"owner": sibling, "helper": outer}, device_id_type=MESH)
            inward_middle(chunks - 1).wait_send()

        @pl.when(is_end)
        def _():
            locate()
            pl.semaphore_wait(turn, 1)
            each_chunk(lambda c: inward_end(c).start())

        each_chunk(self_chunk)

    @pl.when(is_inner)
    def _():
        @pl.when(is_middle)
        def _():
            each_chunk(lambda c: swap_near(c).start())
            each_chunk(lambda c: share_near(c).start())

        @pl.when(is_end)
        def _():
            each_chunk(lambda c: keep(c).start())

        @pl.when(o == 2)
        def _():
            each_chunk(lambda c: keep_part(c).start())

        row_best[...] = jnp.full_like(row_best, FLOOR)
        res_best[...] = jnp.full_like(res_best, FLOOR)
        part_best[...] = jnp.full_like(part_best, FLOOR)

        def locate_all():
            locate()
            res_ids[0:1, :] = located(held * line + near)
            res_ids[1:2, :] = located(held * line + outer)
            shared = (1 + jnp.minimum(o, 1)) * line
            part_ids[0:1, :] = located(shared + near)
            part_ids[1:2, :] = located(shared + outer)
            for slot in range(line):
                locate_rows(slot, held * line + slot)

        def kept(c):
            keep(c).wait()

            @pl.when(gives)
            def _():
                flow(near, c).start()

        @pl.when(is_end)
        def _():
            each_chunk(kept)
            locate_all()
            each_chunk(self_chunk)

        def first(c):
            swap_near(c).wait_recv()

            @pl.when(gives)
            def _():
                flow(near, c).start()

            inward_middle(c).wait_recv()
            swap_outer(c).start()
            share_outer(c).start()
            self_chunk(c)

        @pl.when(is_middle)
        def _():
            locate_all()
            each_chunk(first)

        @pl.when(is_end)
        def _():
            each_chunk(lambda c: share_near(c).wait_recv())

        @pl.when(o == 2)
        def _():
            each_chunk(lambda c: keep_part(c).wait())

        @pl.when(o != 1)
        def _():
            each_group(lambda g: with_part(near, g, 0))

        @pl.when(is_end)
        def _():
            each_chunk(lambda c: share_outer(c).wait_recv())

        @pl.when(takes)
        def _():
            def early(g):
                in_group(g, lambda c: flow(there, c).wait_recv())
                with_res(there, g, 0)

                @pl.when(o != 1)
                def _():
                    with_part(near, g, 1)
                    for which in range(2):
                        with_part(there, g, which)

            each_group(early)

        def relay(c):
            @pl.when(is_middle)
            def _():
                swap_outer(c).wait_recv()

            @pl.when(is_end)
            def _():
                inward_end(c).wait_recv()

            @pl.when(gives)
            def _():
                flow(outer, c).start()

        def late(g):
            in_group(g, relay)
            with_res(outer, g, 0)

            @pl.when(o != 1)
            def _():
                with_part(outer, g, 1)

                @pl.when(gives)
                def _():
                    with_part(outer, g, 0)

        each_group(late)

        @pl.when(takes)
        def _():
            each_group(lambda g: with_res(there, g, 1))
            message[there] = folded(there)
            to_home(there).start()

            def last(g):
                in_group(g, lambda c: flow(there_outer, c).wait_recv())
                for which in range(2):
                    with_res(there_outer, g, which)

                @pl.when(o != 1)
                def _():
                    for which in range(2):
                        with_part(there_outer, g, which)

            each_group(last)
            message[there_outer] = folded(there_outer)
            to_home(there_outer).start()

        message[outer] = jnp.maximum(folded(outer), res_best[1])
        to_home(outer).start()
        message[near] = jnp.maximum(folded(near), res_best[0])

        @pl.when(is_middle)
        def _():
            to_home(near).start()

        @pl.when(is_end)
        def _():
            part_home(0).start()
            part_home(1).start()
            own_best[...] = jnp.maximum(own_best[...], message[near])

        @pl.when(o == 2)
        def _():
            pair_home.start()
            own_best[...] = jnp.maximum(own_best[...], part_best[0])

    @pl.when(is_outer | is_middle)
    def _():
        from_holder(near - 1).wait_recv()
        own_best[...] = jnp.maximum(own_best[...], returned[near - 1])

    @pl.when(near != 1 + held % 2)
    def _():
        from_holder(2 - near).wait_recv()
        own_best[...] = jnp.maximum(own_best[...], returned[2 - near])

    @pl.when(is_middle)
    def _():
        part_home(0).wait_recv()
        own_best[...] = jnp.maximum(own_best[...], part_back[...])

    @pl.when((o == 2) & is_outer)
    def _():
        pair_home.wait_recv()
        own_best[...] = jnp.maximum(own_best[...], pair_back[...])

    out_ref[...] = own_best[...]

    @pl.when(is_outer & is_end)
    def _():
        each_chunk(lambda c: inward_end(c).wait_send())

    @pl.when(is_inner)
    def _():
        to_home(outer).wait_send()

        @pl.when(takes)
        def _():
            to_home(there).wait_send()
            to_home(there_outer).wait_send()

        @pl.when(gives)
        def _():
            each_chunk(lambda c: flow(near, c).wait_send())
            each_chunk(lambda c: flow(outer, c).wait_send())

        @pl.when(is_middle)
        def _():
            to_home(near).wait_send()
            for copy in (swap_near, swap_outer, share_near, share_outer):
                each_chunk(lambda c, copy=copy: copy(c).wait_send())

        @pl.when(is_end)
        def _():
            part_home(0).wait_send()
            part_home(1).wait_send()

        @pl.when(o == 2)
        def _():
            pair_home.wait_send()


def chain_body(line, embeddings, cluster_sizes):
    rows, width = embeddings.shape
    ends = jnp.cumsum(cluster_sizes)
    chunks = rows // CHUNK
    best = pl.pallas_call(
        functools.partial(kernel, line),
        out_shape=jax.ShapeDtypeStruct((8, rows), jnp.float32),
        in_specs=[pl.BlockSpec(memory_space=pltpu.VMEM)] * 3,
        out_specs=pl.BlockSpec(memory_space=pltpu.VMEM),
        scratch_shapes=[
            pltpu.VMEM((rows, width), jnp.bfloat16),
            pltpu.VMEM(((line + 1) * rows, 1), jnp.float32),
            pltpu.VMEM((1, rows), jnp.float32),
            pltpu.VMEM((2, rows), jnp.float32),
            pltpu.VMEM((2, rows), jnp.float32),
            pltpu.VMEM((line, rows, width), jnp.bfloat16),
            pltpu.VMEM((2, rows, width), jnp.bfloat16),
            pltpu.VMEM((line, rows, 128), jnp.float32),
            pltpu.VMEM((2, 8, rows), jnp.float32),
            pltpu.VMEM((2, 8, rows), jnp.float32),
            pltpu.VMEM((8, rows), jnp.float32),
            pltpu.VMEM((line, 8, rows), jnp.float32),
            pltpu.VMEM((2, 8, rows), jnp.float32),
            pltpu.VMEM((8, rows), jnp.float32),
            pltpu.VMEM((8, rows), jnp.float32),
            pltpu.SemaphoreType.DMA((chunks,)),
            pltpu.SemaphoreType.DMA((2, chunks)),
            pltpu.SemaphoreType.DMA((line, chunks)),
            pltpu.SemaphoreType.DMA((2, chunks)),
            pltpu.SemaphoreType.DMA((2, chunks)),
            pltpu.SemaphoreType.DMA((line, chunks)),
            pltpu.SemaphoreType.DMA((line,)),
            pltpu.SemaphoreType.DMA((2,)),
            pltpu.SemaphoreType.DMA((2,)),
            pltpu.SemaphoreType.DMA,
            pltpu.SemaphoreType.DMA,
            pltpu.SemaphoreType.DMA,
            pltpu.SemaphoreType.REGULAR,
        ],
        compiler_params=pltpu.CompilerParams(
            collective_id=0, has_side_effects=True, vmem_limit_bytes=48 * 2**20
        ),
    )(embeddings, ends[None], ends[:, None])
    return jnp.maximum(jnp.max(best, axis=0), -1.0)


def solution(mesh):
    placed = (P(("parts", "owner", "helper"), None), P("parts"))
    line = mesh.shape["helper"]
    chained = mesh.shape["owner"] == 4 and line == REACH
    return jax.shard_map(
        functools.partial(chain_body, line) if chained else body,
        mesh=mesh, in_specs=placed, out_specs=P(("parts", "owner", "helper")), check_vma=False
    )
```
